32 devices in a mesh: dp: 2 (over x), ctx: 4 (over y, core), tensor: 4 (over z).
Axes of the slice: x: 2, y: 2, z: 4, core: 2. Of those that a mesh axis runs over, the one named last changes fastest.
Arguments:
- tokens: bfloat16 [8192, 768], P(('dp', 'ctx', 'tensor')), may hold values from -6 to 6
- lengths: int32 [2, 5], P('dp'), may hold values from 0 to 3892, as said below
- gain_attn: bfloat16 [768], P('dp'), may hold values from 0.099609375 to 1.8984375
- w_qkv: bfloat16 [3, 768, 768], P(None, 'dp', 'tensor'), may hold values from -0.21875 to 0.21875
- w_out: bfloat16 [768, 768], P('tensor', 'dp'), may hold values from -1.75 to 1.75
- gain_mlp: bfloat16 [768], P('dp'), may hold values from 0.099609375 to 1.8984375
- w_in: bfloat16 [2, 768, 1152], P(None, 'dp', 'tensor'), may hold values from -0.21875 to 0.21875
- w_down: bfloat16 [1152, 768], P('tensor', 'dp'), may hold values from -0.1875 to 0.1875
- cotangent: bfloat16 [8192, 768], P(('dp', 'ctx', 'tensor')), may hold values from -6 to 6
Outputs:
- activations: bfloat16 [8192, 768], P(('dp', 'ctx', 'tensor'))
- grad_tokens: bfloat16 [8192, 768], P(('dp', 'ctx', 'tensor'))
- grad_gain_attn: float32 [768], P('dp')
- grad_w_qkv: float32 [3, 768, 768], P(None, 'dp', 'tensor')
- grad_w_out: float32 [768, 768], P('tensor', 'dp')
- grad_gain_mlp: float32 [768], P('dp')
- grad_w_in: float32 [2, 768, 1152], P(None, 'dp', 'tensor')
- grad_w_down: float32 [1152, 768], P('tensor', 'dp')
The draws below stay inside these ranges and needn't reach their ends.
Inputs may be any that keep to these rules, and one draw needn't show every extreme that they name: Row s lists in order the lengths of the documents packed into sequence s, followed by zeros where it has fewer than 5; each row sums to 4096; each row holds one document longer than 3072, and its other documents have 1024 // 5 to 255 tokens (at least 1).
All inputs are finite; a program needn't handle non-finite values.
Results may differ from the reference program's by a relative error of at most 0.025.
Values may be sent and summed in bfloat16 or wider, within the bound.
No kernel may reach another device: no remote copies, remote signals or barrier semaphores. Data moves between devices by JAX's collectives and lax.ppermute only.
A program may use at most 128 MiB of HBM per device.

```python
import math
from functools import partial
import jax
import jax.numpy as jnp
from jax import lax

HEADS = 12
HEAD_DIM = 64
D = 768
FF = 1152
SEQUENCE_TOKENS = 1024
DOCS = 5
SEQ_LEN = 4096
SEQS = 2
TOKENS = 8192


def draw_lengths(key, part):
    key = jax.random.fold_in(key, 11)
    short_key, count_key, place_key = jax.random.split(key, 3)
    short_low = max(1, SEQUENCE_TOKENS // 5)
    short_top = max(short_low, (SEQUENCE_TOKENS - 1) // (DOCS - 1))
    row_ids = jnp.arange(SEQS, dtype=jnp.int32)[:, None]
    column = jnp.arange(DOCS, dtype=jnp.int32)[None, :]
    counts = jax.random.randint(count_key, (SEQS, 1), 1, DOCS).astype(jnp.int32)
    counts = jnp.where(row_ids == 0, 1, counts).astype(jnp.int32)
    raw_shorts = jax.random.randint(short_key, (SEQS, DOCS - 1), short_low, short_top + 1).astype(jnp.int32)
    raw_shorts = jnp.where(row_ids == 0, short_low, raw_shorts).astype(jnp.int32)
    short_cols = jnp.arange(DOCS - 1, dtype=jnp.int32)[None, :]
    shorts = jnp.where(short_cols < counts, raw_shorts, 0).astype(jnp.int32)
    longest = (SEQ_LEN - jnp.sum(shorts, axis=1)).astype(jnp.int32)
    placement_order = jax.random.randint(place_key, (SEQS, 1), 0, counts + 1).astype(jnp.int32)
    filler = jnp.zeros((SEQS, 1), jnp.int32)
    before = jnp.concatenate([shorts, filler], axis=1)
    trailing = jnp.concatenate([filler, shorts], axis=1)
    chosen = jnp.where(column < placement_order, before, jnp.where(column == placement_order, longest[:, None], trailing))
    return chosen.astype(jnp.int32)


def level_of(stream_key, extent, cuts, smallest, largest):
    factor_of, own = 1.0, jax.random.fold_in(stream_key, 6)
    for position, parts in cuts:
        steps = jnp.exp(jax.random.uniform(jax.random.fold_in(own, position), (parts,), jnp.float32, smallest / len(cuts), largest / len(cuts)))
        factor_of = factor_of * jnp.repeat(steps, extent[position] // parts).reshape([-1 if axis == position else 1 for axis in range(len(extent))])
    return factor_of


def centred(rng, extent, deviation, limit, shards=(), kind=jnp.bfloat16):
    level = level_of(rng, extent, shards, -0.22, 0.18) if shards else 1.0
    drawn = jax.random.normal(rng, extent, jnp.float32) * deviation * level
    return jnp.minimum(jnp.maximum(drawn, -limit), limit).astype(kind)


def setup_inputs(seed: int = 0) -> dict:
    key_of = jax.random.split(jax.random.key(seed), 10)
    tokens = centred(key_of[0], (TOKENS, D), 1.0, 6.0, ((0, 32),))
    lengths = draw_lengths(jax.random.fold_in(key_of[9], 71), 0)
    gain_attn = jnp.clip(1.0 + 0.18 * jax.random.normal(key_of[2], (D,), jnp.float32), 0.099609375, 1.8984375).astype(jnp.bfloat16)
    w_qkv = centred(key_of[3], (3, D, D), D ** -0.5, 0.21875, ((1, 2), (2, 4)))
    w_out = centred(key_of[4], (D, D), (max(1, D // 64)) ** -0.5, 1.75, ((0, 4), (1, 2)))
    gain_mlp = jnp.clip(1.0 + 0.18 * jax.random.normal(key_of[5], (D,), jnp.float32), 0.099609375, 1.8984375).astype(jnp.bfloat16)
    w_in = centred(key_of[6], (2, D, FF), D ** -0.5, 0.21875, ((1, 2), (2, 4)))
    w_down = centred(key_of[7], (FF, D), FF ** -0.5, 0.1875, ((0, 4), (1, 2)))
    cotangent = centred(key_of[8], (TOKENS, D), 1.0, 6.0, ((0, 32),))
    return dict(tokens=tokens, lengths=lengths, gain_attn=gain_attn, w_qkv=w_qkv, w_out=w_out, gain_mlp=gain_mlp, w_in=w_in, w_down=w_down, cotangent=cotangent)


EPSILON = 1e-05
ROPE_BASE = 160000.0
MASKED = -1e+30
HIGHEST = lax.Precision.HIGHEST

@jax.custom_vjp
def low(v):
    return lax.optimization_barrier(v.astype(jnp.bfloat16)).astype(jnp.float32)

@jax.custom_vjp
def low_back(v):
    return v

def low_keep(v):
    return (low(v), None)

def low_pass(kept, grad):
    return (grad,)

def back_keep(v):
    return (v, None)

def back_low(kept, grad):
    return (low(grad),)
low.defvjp(low_keep, low_pass)
low_back.defvjp(back_keep, back_low)

def segment_of(positions, doc_lengths):
    bounds = jnp.cumsum(doc_lengths)
    return lax.optimization_barrier(jnp.sum((positions[:, None] >= bounds[None, :]).astype(jnp.int32), axis=1)).astype(jnp.int32)

def rope_tables(positions):
    halves = HEAD_DIM // 2
    exponent = jnp.arange(halves, dtype=jnp.float32) * (2.0 / HEAD_DIM)
    inverse = ROPE_BASE ** (-exponent)
    angles = positions.astype(jnp.float32)[:, None] * inverse[None, :]
    return (jnp.cos(angles), jnp.sin(angles))

def rotate(values, cosine, sine_table):
    halves = values.shape[-1] // 2
    first = values[..., :halves]
    second = values[..., halves:]
    cos_wide = cosine[:, None, :]
    sin_wide = sine_table[:, None, :]
    return jnp.concatenate([first * cos_wide - second * sin_wide, second * cos_wide + first * sin_wide], axis=-1)

def layer_norm(values, gain):
    centre = values - lax.optimization_barrier(jnp.mean(values, axis=-1, keepdims=True))
    spread = lax.optimization_barrier(jnp.mean(centre * centre, axis=-1, keepdims=True))
    return centre * lax.rsqrt(spread + EPSILON) * gain

def gelu_exact(values):
    return jax.nn.gelu(values, approximate=False)

def layer(inputs, gain_attn, w_qkv, w_out, gain_mlp, w_in, w_down, segments):
    length = inputs.shape[0]
    normed = low(layer_norm(inputs, gain_attn))
    project = jnp.einsum('sd,tdc->tsc', normed, w_qkv, precision=HIGHEST)
    positions = jnp.arange(length, dtype=jnp.int32)
    cosine, sine_table = rope_tables(positions)
    head_shape = (length, HEADS, HEAD_DIM)
    queries = low(rotate(low_back(project[0]).reshape(head_shape), cosine, sine_table))
    keys_rot = low(rotate(low_back(project[1]).reshape(head_shape), cosine, sine_table))
    values = low(low_back(project[2])).reshape(head_shape)
    block_row_span = math.gcd(length, 512)
    block_count = length // block_row_span
    score_scale = HEAD_DIM ** (-0.5)

    def attend(block_pair):
        query_block, segment_block = block_pair
        scores = jnp.einsum('qhd,khd->hqk', query_block, keys_rot, precision=HIGHEST) * score_scale
        scores = low_back(scores)
        same_doc = segment_block[:, None] == segments[None, :]
        scores = jnp.where(same_doc[None], scores, MASKED)
        maxima = lax.optimization_barrier(jnp.max(scores, axis=-1, keepdims=True))
        logsum = maxima + jnp.log(lax.optimization_barrier(jnp.sum(jnp.exp(scores - maxima), axis=-1, keepdims=True)))
        probs_low = low(jnp.exp(scores - logsum))
        return jnp.einsum('hqk,khd->qhd', probs_low, values, precision=HIGHEST)
    mixed_heads = lax.map(jax.checkpoint(attend), (queries.reshape(block_count, block_row_span, HEADS, HEAD_DIM), segments.reshape(block_count, block_row_span)))
    heads_out = low(low_back(mixed_heads.reshape(length, HEADS * HEAD_DIM)))
    attended = low_back(jnp.dot(heads_out, w_out, precision=HIGHEST))
    hidden = inputs + attended
    normed_two = low(layer_norm(hidden, gain_mlp))
    inner_out = low_back(jnp.einsum('sd,tdf->tsf', normed_two, w_in, precision=HIGHEST))
    product = low(gelu_exact(inner_out[0]) * inner_out[1])
    branch = low_back(jnp.dot(product, w_down, precision=HIGHEST))
    return hidden + branch

def reference(tokens, lengths, gain_attn, w_qkv, w_out, gain_mlp, w_in, w_down, cotangent):
    parameter_set = (gain_attn.astype(jnp.float32), w_qkv.astype(jnp.float32), w_out.astype(jnp.float32), gain_mlp.astype(jnp.float32), w_in.astype(jnp.float32), w_down.astype(jnp.float32))
    inputs = tokens.astype(jnp.float32).reshape(SEQS, SEQ_LEN, D)
    cotangents = cotangent.astype(jnp.float32).reshape(SEQS, SEQ_LEN, D)

    def one_sequence(totals, sequence):
        rows, grads_out, doc_lengths = sequence
        segments = segment_of(jnp.arange(SEQ_LEN, dtype=jnp.int32), doc_lengths)
        result, backward = jax.vjp(partial(layer, segments=segments), rows, parameter_set[0], parameter_set[1], parameter_set[2], parameter_set[3], parameter_set[4], parameter_set[5])
        grads = backward(grads_out)
        totals = tuple((summed + update for summed, update in zip(totals, grads[1:])))
        return (totals, (result.astype(jnp.bfloat16), grads[0].astype(jnp.bfloat16)))
    initial = tuple((jnp.zeros(parameter.shape, jnp.float32) for parameter in parameter_set))
    totals, (outputs, input_grads) = lax.scan(one_sequence, initial, (inputs, cotangents, lengths))
    return (outputs.reshape(TOKENS, D), input_grads.reshape(TOKENS, D), totals[0], totals[1], totals[2], totals[3], totals[4], totals[5])
```

```python
import functools

import jax
import jax.numpy as jnp
from jax import lax
from jax.experimental import pallas as pl
from jax.experimental.pallas import tpu as pltpu
from jax.sharding import PartitionSpec as P

HD = 64
CTX = 4
TENSOR = 4
EPSILON = 1e-05
ROPE_BASE = 160000.0
MASKED = -1e30
LOG2E = 1.4426950408889634
NN = (((1,), (0,)), ((), ()))
NT = (((1,), (1,)), ((), ()))
TN = (((0,), (0,)), ((), ()))


def mm(a, b, dims=NN):
    return lax.dot_general(a, b, dims, preferred_element_type=jnp.float32)


def fwd_body(blocks, first, last, *refs):
    q_ref, mq_ref = refs[:2]
    kv_refs, mk_refs = refs[2 : 2 + blocks], refs[2 + blocks : 2 + 2 * blocks]
    rest = refs[2 + 2 * blocks :]
    rows = q_ref.shape[2]
    qb = min(rows, 512)
    if not first:
        m_in, acc_in, *rest = rest
    if last:
        out_ref, lse_ref, *rest = rest
    m_ref, acc_ref = rest
    if first:
        m_ref[...] = jnp.full_like(m_ref, MASKED)
        acc_ref[...] = jnp.zeros_like(acc_ref)
    else:
        m_ref[...] = m_in[...]
        acc_ref[...] = acc_in[...]
    for kv_ref, mk_ref in zip(kv_refs, mk_refs):
        keys = jnp.concatenate([kv_ref[0, :HD], mk_ref[...]], axis=0).T
        vals = jnp.concatenate([kv_ref[0, HD:], jnp.ones((16, rows), jnp.bfloat16)], axis=0)
        for j in range(rows // qb):
            at = slice(j * qb, (j + 1) * qb)
            right = jnp.concatenate([q_ref[0, :, at], mq_ref[:, at]], axis=0)
            s = mm(keys, right)
            old = m_ref[0, :, at]
            new = jnp.maximum(old, jnp.max(s, axis=0, keepdims=True))
            p = jnp.exp2(s - new).astype(jnp.bfloat16)
            acc_ref[0, :, at] = acc_ref[0, :, at] * jnp.exp2(old - new) + mm(vals, p)
            m_ref[0, :, at] = new
    if last:
        total = acc_ref[0, HD : HD + 1]
        out_ref[0] = acc_ref[0, :HD] / total
        lse_ref[0] = m_ref[0] + jnp.log2(total)


def per_head(a, b):
    return pl.BlockSpec((1, a, b), lambda h: (h, 0, 0))


def same(a, b):
    return pl.BlockSpec((a, b), lambda h: (0, 0))


def cost(heads, rows, keys, products):
    return pl.CostEstimate(
        flops=heads * rows * keys * HD * products * 8,
        bytes_accessed=4 * 2**20,
        transcendentals=heads * rows * keys,
    )


def attn_fwd(q, mq, kv, mk, state=None, last=False):
    heads, _, rows = q.shape
    blocks = len(kv)
    carried = [per_head(1, rows), per_head(HD + 16, rows)]
    result = [per_head(HD, rows), per_head(1, rows)]
    shape = lambda a: jax.ShapeDtypeStruct((heads, a, rows), jnp.float32)
    first = state is None
    return pl.pallas_call(
        functools.partial(fwd_body, blocks, first, last),
        grid=(heads,),
        in_specs=[per_head(HD, rows), same(HD, rows)]
        + [per_head(2 * HD, rows)] * blocks
        + [same(HD, rows)] * blocks
        + ([] if first else carried),
        out_specs=result if last else carried,
        out_shape=[shape(HD), shape(1)] if last else [shape(1), shape(HD + 16)],
        scratch_shapes=[]
        if not last
        else [pltpu.VMEM((1, 1, rows), jnp.float32), pltpu.VMEM((1, HD + 16, rows), jnp.float32)],
        compiler_params=pltpu.CompilerParams(vmem_limit_bytes=40 * 2**20),
        cost_estimate=cost(heads, rows, rows * blocks, 2),
        name="attend",
    )(q, mq, *kv, *mk, *(() if first else state))


def bwd_body(blocks, more, *refs):
    q_ref, mq_ref = refs[:2]
    kv_refs, mk_refs = refs[2 : 2 + blocks], refs[2 + blocks : 2 + 2 * blocks]
    lse_ref, do_ref, dl_ref, *rest = refs[2 + 2 * blocks :]
    if more:
        dq_in, dq_ref, *dkv_refs = rest
        dq_ref[...] = dq_in[...]
    else:
        dq_ref, *dkv_refs = rest
        dq_ref[...] = jnp.zeros_like(dq_ref)
    rows = q_ref.shape[2]
    qb = min(rows, 512)
    for kv_ref, mk_ref, dkv_ref in zip(kv_refs, mk_refs, dkv_refs):
        kt = kv_ref[0, :HD]
        keys = jnp.concatenate([kt, mk_ref[...]], axis=0).T
        vals = kv_ref[0, HD:].T
        dk = jnp.zeros((HD, rows), jnp.float32)
        dv = jnp.zeros((HD, rows), jnp.float32)
        for j in range(rows // qb):
            at = slice(j * qb, (j + 1) * qb)
            qj = q_ref[0, :, at]
            doj = do_ref[0, :, at]
            s = mm(keys, jnp.concatenate([qj, mq_ref[:, at]], axis=0))
            p = jnp.exp2(s - lse_ref[0, :, at])
            dp = mm(vals, doj)
            ds = (p * (dp - dl_ref[0, :, at])).astype(jnp.bfloat16)
            dv = dv + mm(doj, p.astype(jnp.bfloat16), NT)
            dk = dk + mm(qj, ds, NT)
            dq_ref[0, :, at] += mm(kt, ds)
        dkv_ref[0, :HD] = (dk * (1.0 / LOG2E)).astype(jnp.bfloat16)
        dkv_ref[0, HD:] = dv.astype(jnp.bfloat16)


def attn_bwd(q, mq, kv, mk, lse, do, delta, dq=None):
    heads, _, rows = q.shape
    blocks = len(kv)
    more = dq is not None
    out = pl.pallas_call(
        functools.partial(bwd_body, blocks, more),
        grid=(heads,),
        in_specs=[per_head(HD, rows), same(HD, rows)]
        + [per_head(2 * HD, rows)] * blocks
        + [same(HD, rows)] * blocks
        + [per_head(1, rows), per_head(HD, rows), per_head(1, rows)]
        + ([per_head(HD, rows)] if more else []),
        out_specs=[per_head(HD, rows)] + [per_head(2 * HD, rows)] * blocks,
        out_shape=[jax.ShapeDtypeStruct((heads, HD, rows), jnp.float32)]
        + [jax.ShapeDtypeStruct((heads, 2 * HD, rows), jnp.bfloat16)] * blocks,
        compiler_params=pltpu.CompilerParams(vmem_limit_bytes=40 * 2**20),
        cost_estimate=cost(heads, rows, rows * blocks, 5),
        name="attend_back",
    )(q, mq, *kv, *mk, lse, do, delta, *((dq,) if more else ()))
    return out[0], out[1:]


def swap(x, axis, size, d):
    return lax.ppermute(x, axis, [(i, i ^ d) for i in range(size)])


def norm_parts(values):
    centre = values - jnp.mean(values, axis=-1, keepdims=True)
    spread = jnp.mean(centre * centre, axis=-1, keepdims=True)
    scaling = lax.rsqrt(spread + EPSILON)
    return centre * scaling, scaling


def norm_back(scaled, normal, scaling):
    return scaling * (
        scaled
        - jnp.mean(scaled, axis=-1, keepdims=True)
        - normal * jnp.mean(scaled * normal, axis=-1, keepdims=True)
    )


def low(x):
    return x.astype(jnp.bfloat16)


def wide(x):
    return x.astype(jnp.float32)


def together(*values):
    return lax.optimization_barrier(values)


def local(dp, tokens, lengths, gain_attn, w_qkv, w_out, gain_mlp, w_in, w_down, cotangent):
    share, width = tokens.shape
    group = w_out.shape[0]
    heads = group // HD
    units = w_down.shape[0]
    half = w_out.shape[1]
    rows = share * TENSOR
    ctx = lax.axis_index("ctx")
    tensor = lax.axis_index("tensor")
    dp_index = lax.axis_index("dp")
    core, chip = ctx % 2, ctx // 2

    def gather_dp(x):
        if dp != 2:
            return lax.all_gather(x, "dp", axis=x.ndim - 1, tiled=True)
        other = swap(x, "dp", 2, 1)
        first = dp_index == 0
        return jnp.concatenate([jnp.where(first, x, other), jnp.where(first, other, x)], -1)

    def sum_dp(x):
        if dp != 2:
            return wide(lax.psum_scatter(low(x), "dp", scatter_dimension=x.ndim - 1, tiled=True))
        mine = lax.dynamic_slice_in_dim(x, dp_index * half, half, x.ndim - 1)
        theirs = lax.dynamic_slice_in_dim(x, (1 - dp_index) * half, half, x.ndim - 1)
        return wide(mine) + wide(swap(low(theirs), "dp", 2, 1))

    def over_z(x):
        return [x] + [swap(x, "tensor", TENSOR, d) for d in (1, 2, 3)]

    def pair_gather(x, bit, d, axis):
        other = swap(x, "ctx", CTX, d)
        return jnp.concatenate(
            [jnp.where(bit == 0, x, other), jnp.where(bit == 0, other, x)], axis
        )

    def pair_sum(x, bit, d, axis):
        mine = lax.dynamic_index_in_dim(x, bit, axis, False)
        theirs = lax.dynamic_index_in_dim(x, 1 - bit, axis, False)
        return wide(mine) + wide(swap(low(theirs), "ctx", CTX, d))

    def by_chip(x):
        return pair_gather(x[:, None], chip, 2, 1)

    def by_core(x):
        n, _, r, w = x.shape
        return pair_gather(x[:, :, None], core, 1, 2).reshape(n, CTX, r, w)

    def quarter(x):
        r = x.shape[-2] // 4
        return lax.dynamic_slice_in_dim(x, ctx * r, r, x.ndim - 2)

    token_parts = over_z(tokens)
    qkv_shard = jnp.swapaxes(w_qkv, 1, 2).reshape(3 * group, half)
    packed = jnp.concatenate([qkv_shard, gain_attn[None], gain_mlp[None]], 0)
    packed = gather_dp(packed)
    qkv_own = packed[: 3 * group]
    gain_one, gain_two = wide(packed[3 * group]), wide(packed[3 * group + 1])
    inputs = wide(tokens)

    g, n = group // CTX, units // CTX
    in_turned = jnp.swapaxes(w_in, 1, 2)
    quarters = [quarter(w_out), quarter(in_turned[0]), quarter(in_turned[1]), quarter(w_down)]
    quarters = jnp.concatenate(quarters, 0)

    normed_parts = []
    for part in token_parts:
        normal, _ = norm_parts(wide(part))
        normed_parts.append(low(normal * gain_one))
    quarters, *normed_parts = together(quarters, *normed_parts)
    weights = over_z(quarters)
    normed = jnp.concatenate(normed_parts, 0)
    project = jnp.concatenate([mm(qkv_own, part, NT) for part in normed_parts], 1)
    project = project.reshape(3, heads, HD, rows)

    block = jnp.arange(rows, dtype=jnp.int32) // share
    place = (block ^ tensor) * share + jnp.arange(rows, dtype=jnp.int32) % share
    bounds = jnp.cumsum(lengths[0])

    def segments(e):
        at = (ctx ^ e) * rows + place
        return jnp.sum((at[None, :] >= bounds[:, None]).astype(jnp.int32), axis=0)

    feature = lax.broadcasted_iota(jnp.int32, (HD, rows), 0)

    def key_mask(e):
        return (feature == segments(e)[None, :]).astype(jnp.bfloat16)

    query_mask = jnp.where(
        (feature == segments(0)[None, :]) | (feature >= lengths.shape[1]), 0.0, MASKED
    ).astype(jnp.bfloat16)
    exponent = jnp.arange(HD // 2, dtype=jnp.float32) * (2.0 / HD)
    angles = (ROPE_BASE ** (-exponent))[:, None] * (ctx * rows + place).astype(jnp.float32)[None, :]
    cosine, sine = jnp.cos(angles), jnp.sin(angles)

    def rotate(x, sine):
        a, b = x[:, : HD // 2], x[:, HD // 2 :]
        return jnp.concatenate([a * cosine - b * sine, b * cosine + a * sine], 1)

    queries = low(rotate(project[0], sine) * (HD**-0.5 * LOG2E))
    kv = jnp.concatenate([low(rotate(project[1], sine)), low(project[2])], 1)
    kv_core = swap(kv, "ctx", CTX, 1)
    kv_chip = swap(kv, "ctx", CTX, 2)

    ask = (queries, query_mask)
    state = attn_fwd(*ask, [kv], [key_mask(0)])
    *state, kv_core = together(*state, kv_core)
    state = attn_fwd(*ask, [kv_core], [key_mask(1)], state=state)
    *state, weights[1], weights[2], weights[3], kv_chip = together(*state, *weights[1:], kv_chip)
    weights_a = gather_dp(jnp.stack(weights[:2]))
    weights_b = by_chip(jnp.stack(weights[2:]))
    qkv_full = over_z(together(quarter(qkv_own), state[0])[0])
    kv_far = swap(kv_chip, "ctx", CTX, 1)
    far = ([kv_chip, kv_far], [key_mask(2), key_mask(3)])
    heads_out, logsum = attn_fwd(*ask, *far, state=state, last=True)
    heads_out, logsum, weights_a, weights_b, *qkv_full = together(
        heads_out, logsum, weights_a, weights_b, *qkv_full
    )
    heads_low = low(heads_out).reshape(group, rows)
    heads_own = jnp.concatenate(
        [heads_low[:, :share]]
        + [
            swap(heads_low[:, d * share : (d + 1) * share], "tensor", TENSOR, d)
            for d in (1, 2, 3)
        ],
        0,
    )

    weights_a = by_core(by_chip(weights_a))
    weights_b = by_core(gather_dp(weights_b))
    weights = jnp.concatenate([weights_a, weights_b], 0)
    out_full = weights[:, :, :g].reshape(-1, width)
    in_full = [weights[:, :, g + t * n : g + (t + 1) * n].reshape(-1, width) for t in (0, 1)]
    down_full = weights[:, :, g + 2 * n :].reshape(-1, width)
    heads_own, out_full, *in_full, down_full = together(heads_own, out_full, *in_full, down_full)
    qkv_full = by_chip(jnp.stack(qkv_full))
    hidden = inputs + mm(heads_own, out_full, TN)
    normal_two, scaling_two = norm_parts(hidden)
    normed_two = low(normal_two * gain_two)
    inner = [mm(in_full[t], normed_two, NT) for t in (0, 1)]
    activated, gelu_back = jax.vjp(lambda v: jax.nn.gelu(v, approximate=False), inner[0])
    product = low(activated * inner[1])
    grad_product = mm(down_full, cotangent, NT)
    grad_inner = [
        low(gelu_back(grad_product * inner[1])[0]),
        low(grad_product * activated),
    ]
    grad_normed_two = sum(mm(grad_inner[t], in_full[t], TN) for t in (0, 1))
    grad_hidden = wide(cotangent) + norm_back(grad_normed_two * gain_two, normal_two, scaling_two)
    grad_hidden_low = low(grad_hidden)
    grad_heads_own = low(mm(out_full, grad_hidden_low, NT))
    grad_heads_own, qkv_full = together(grad_heads_own, qkv_full)
    grad_heads_own = grad_heads_own.reshape(TENSOR, group, share)
    grad_heads = [grad_heads_own[0]] + [
        swap(grad_heads_own[d], "tensor", TENSOR, d) for d in (1, 2, 3)
    ]

    gain_sum = low(jnp.sum(grad_normed_two * normal_two, axis=0))
    gain_sum = jnp.broadcast_to(gain_sum, (TENSOR, 2, 8, width))

    def gradients(bit):
        def rows_of(x):
            x = x.reshape(TENSOR, 2, 2, -1, share)
            return lax.dynamic_index_in_dim(x, bit, 2, False).reshape(-1, share)

        def against(x, y):
            return low(mm(rows_of(x), y)).reshape(TENSOR, 2, -1, width)

        return jnp.concatenate(
            [
                against(heads_own, grad_hidden_low),
                against(grad_inner[0], normed_two),
                against(grad_inner[1], normed_two),
                against(product, cotangent),
                gain_sum,
            ],
            2,
        )

    theirs = swap(gradients(1 - core), "ctx", CTX, 1)
    grad_all = low(wide(gradients(core)) + wide(theirs))
    *grad_heads, grad_all = together(*grad_heads, grad_all)
    grad_heads = jnp.concatenate(grad_heads, 1).reshape(heads, HD, rows)
    part_a = pair_sum(grad_all[:2], chip, 2, 1)
    part_b = sum_dp(grad_all[2:])

    delta = jnp.sum(wide(grad_heads) * heads_out, axis=1, keepdims=True)
    given = (logsum, grad_heads, delta)
    grad_q, (grad_chip, grad_far) = attn_bwd(*ask, *far, *given)
    grad_q, grad_chip, grad_far, part_a, part_b = together(
        grad_q, grad_chip, grad_far, part_a, part_b
    )
    from_core = swap(grad_far, "ctx", CTX, 1)
    from_chip = swap(low(wide(grad_chip) + wide(from_core)), "ctx", CTX, 2)
    part_a = sum_dp(part_a)
    part_b = pair_sum(part_b, chip, 2, 1)
    grad_q, (grad_core,) = attn_bwd(*ask, [kv_core], [key_mask(1)], *given, dq=grad_q)
    grad_q, grad_core, part_a, part_b = together(grad_q, grad_core, part_a, part_b)
    parts = [part_a[0], low(part_a[1]), low(part_b[0]), low(part_b[1])]
    parts[1:] = [swap(parts[d], "tensor", TENSOR, d) for d in (1, 2, 3)]
    from_pair = swap(grad_core, "ctx", CTX, 1)
    grad_q, (grad_kv,) = attn_bwd(*ask, [kv], [key_mask(0)], *given, dq=grad_q)
    grad_q, grad_kv, from_pair, from_chip = together(grad_q, grad_kv, from_pair, from_chip)
    grad_kv = wide(grad_kv) + wide(from_pair) + wide(from_chip)
    grad_project = jnp.stack(
        [
            low(rotate(grad_q * HD**-0.5, -sine)),
            low(rotate(grad_kv[:, :HD], -sine)),
            low(grad_kv[:, HD:]),
        ]
    ).reshape(3 * group, rows)
    grad_project, *parts = together(grad_project, *parts)
    own_project = jnp.concatenate(
        [grad_project[:, :share]]
        + [
            swap(grad_project[:, d * share : (d + 1) * share], "tensor", TENSOR, d)
            for d in (1, 2, 3)
        ],
        0,
    )
    qkv_full = by_core(qkv_full).reshape(-1, width)
    grad_normed = mm(own_project, qkv_full, TN)
    normal_one, scaling_one = norm_parts(inputs)
    grad_inputs = grad_hidden + norm_back(grad_normed * gain_one, normal_one, scaling_one)
    grad_tokens = low(grad_inputs)

    grad_qkv = low(mm(grad_project, normed)).reshape(2, 2, -1, width)
    grad_qkv = sum_dp(pair_sum(low(pair_sum(grad_qkv, core, 1, 1)), chip, 2, 0))
    gain_sum = jnp.sum(grad_qkv * wide(quarter(qkv_shard)), axis=0, keepdims=True)
    gain_sum = sum(over_z(gain_sum))
    grad_qkv = jnp.concatenate([grad_qkv, jnp.broadcast_to(gain_sum, (16, half))], 0)
    grad_qkv = wide(by_core(by_chip(low(grad_qkv)[None])))[0]
    grad_gain_attn = jnp.sum(grad_qkv[:, -1], axis=0) / wide(gain_attn)
    grad_qkv = grad_qkv[:, :-16].reshape(3, group, half)

    grad_all = sum(wide(p) for p in parts)
    grad_all = wide(by_core(by_chip(low(grad_all)[None])))[0]
    grad_out = grad_all[:, :g].reshape(group, half)
    grad_in = jnp.stack(
        [grad_all[:, g + t * n : g + (t + 1) * n].reshape(units, half) for t in (0, 1)]
    )
    grad_down = grad_all[:, g + 2 * n : g + 3 * n].reshape(units, half)
    grad_gain_mlp = grad_all[0, g + 3 * n]
    activations = low(hidden + mm(product, down_full, TN))

    return (
        activations,
        grad_tokens,
        grad_gain_attn,
        wide(jnp.swapaxes(grad_qkv, 1, 2)),
        grad_out,
        grad_gain_mlp,
        jnp.swapaxes(grad_in, 1, 2),
        grad_down,
    )


def solution(mesh):
    rows = P(("dp", "ctx", "tensor"), None)
    weights = (P(None, "dp", "tensor"), P("tensor", "dp"))
    return jax.shard_map(
        functools.partial(local, mesh.shape["dp"]),
        mesh=mesh,
        in_specs=(rows, P("dp", None), P("dp"), *weights, P("dp"), *weights, rows),
        out_specs=(rows, rows, P("dp"), *weights, P("dp"), *weights),
        check_vma=False,
    )
```
